128 devices in a mesh: group: 4 (over z_hi, core), head: 32 (over x, y, z_lo).
Axes of the slice: x: 4, y: 4, z: 4 (z_hi: 2, z_lo: 2; z = z_hi * 2 + z_lo), core: 2. Of those that a mesh axis runs over, the one named last changes fastest.
Arguments:
- queries: bfloat16 [4, 4096, 4096], P('group', 'head')
- keys: bfloat16 [4, 4096, 4096], P('group', 'head')
- values: bfloat16 [4, 4096, 4096], P('group', 'head'), may hold values from -6 to 6
- group_mask: int32 [4, 4, 32], replicated, may hold values from 0 to 1, as said below
- noise_level: int32 [4], replicated, may hold values from 0 to 7
- token_count: int32 [4], replicated, may hold values from 2048 to 4096, as said below
- level_gate: float32 [8, 4096], replicated, may hold values from 0.5 to 2
Outputs:
- gated: bfloat16 [4, 4096, 4096], P('group', 'head')
The draws below stay inside these ranges and needn't reach their ends.
Inputs may be any that keep to these rules, and one draw needn't show every extreme that they name: group_mask[c, c, h] = 1; group_mask[c, e, h] = 0 where e > c or c - e >= 3; the last group attends in every head to all 3 groups it may. `token_count`: some group has all 4096 tokens live.
All inputs are finite; a program needn't handle non-finite values.
Results may differ from the reference program's by a relative error of at most 0.0048.
Values may be sent and summed in bfloat16 or wider, within the bound.
No kernel may reach another device: no remote copies, remote signals or barrier semaphores. Data moves between devices by JAX's collectives and lax.ppermute only.
A program may use at most 128 MiB of HBM per device.

```python
import jax
import jax.numpy as jnp
from jax import lax

HEADS = 32
HD = 128
HH = 4096
GROUPS = 4
SEQ = 4096
WIN = 3
LEVELS = 8


def draw_queries(key, part):
    key = jax.random.fold_in(key, 11)
    drawn = jax.random.normal(key, (GROUPS, SEQ, HEADS * HD), jnp.float32)
    return drawn.astype(jnp.bfloat16)


def draw_keys(key, part):
    key = jax.random.fold_in(key, 12)
    drawn = jax.random.normal(key, (GROUPS, SEQ, HEADS * HD), jnp.float32)
    return drawn.astype(jnp.bfloat16)


def draw_group_mask(key, part):
    key = jax.random.fold_in(key, 21)
    random_bits = jax.random.randint(key, (GROUPS, GROUPS, HEADS), 0, 2)
    rows = jnp.arange(GROUPS)[:, None, None]
    columns = jnp.arange(GROUPS)[None, :, None]
    lagged = rows - columns
    inside = (lagged >= 1) & (lagged < WIN)
    result = jnp.where(lagged == 0, 1, jnp.where(inside, random_bits, 0))
    result = jnp.where((rows == GROUPS - 1) & inside, 1, result)
    return result.astype(jnp.int32)


def draw_token_count(key, part):
    key = jax.random.fold_in(key, 31)
    counted = jax.random.randint(key, (GROUPS,), SEQ // 2, SEQ + 1)
    filled = jax.random.randint(jax.random.fold_in(key, 1), (), 0, GROUPS)
    return jnp.where(jnp.arange(GROUPS) == filled, SEQ, counted).astype(jnp.int32)


def place_ends(values, key, smallest, top_value):
    shape = values.shape
    spot = [jax.random.randint(jax.random.fold_in(key, axis), (), 0, shape[axis]) for axis in range(len(shape))]
    values = values.at[tuple(spot)].set(smallest)
    longest = shape.index(max(shape))
    spot[longest] = (spot[longest] + 1) % shape[longest]
    return values.at[tuple(spot)].set(top_value)


def block_levels(rng, dims, pieces, least, high):
    loudness = 1.0
    for dim, blocks in pieces:
        draws = jax.random.uniform(jax.random.fold_in(jax.random.fold_in(rng, 6), dim), (blocks,), jnp.float32, least / len(pieces), high / len(pieces))
        loudness = loudness * jnp.repeat(jnp.exp(draws), dims[dim] // blocks).reshape((-1,) + (1,) * (len(dims) - 1 - dim))
    return loudness


def centred(rng, extent, spread, most, cuts=(), held_as=jnp.bfloat16):
    values = spread * jax.random.normal(rng, extent, jnp.float32)
    if cuts:
        values = values * block_levels(rng, extent, cuts, -0.22, 0.18)
    return jnp.clip(values, -most, most).astype(held_as)


def setup_inputs(seed: int = 0) -> dict:
    splits = jax.random.split(jax.random.key(seed), 8)
    return {
        "queries": draw_queries(jax.random.fold_in(splits[7], 71), 0),
        "keys": draw_keys(jax.random.fold_in(splits[7], 71), 0),
        "values": centred(splits[2], (GROUPS, SEQ, HH), 1.0, 6.0, ((0, 4), (1, 32))),
        "group_mask": draw_group_mask(jax.random.fold_in(splits[7], 71), 0),
        "noise_level": place_ends(jax.random.randint(splits[4], (GROUPS,), 0, LEVELS), jax.random.fold_in(splits[4], 1), 0, LEVELS - 1).astype(jnp.int32),
        "token_count": draw_token_count(jax.random.fold_in(splits[7], 71), 0),
        "level_gate": jnp.clip(jax.random.uniform(splits[6], (LEVELS, HH), jnp.float32, 0.5, 2.0), 0.5, 2.0),
    }


NEG = -1e30


def block_stats(query_rows, key_rows, value_rows, valid_keys, active):
    scores = jnp.dot(query_rows, key_rows.T, preferred_element_type=jnp.float32) * (HD ** -0.5)
    scores = jnp.where(valid_keys[None, :], scores, NEG)
    block_max = jnp.max(scores, axis=1)
    weights = jnp.where(valid_keys[None, :], jnp.exp(scores - block_max[:, None]), 0.0)
    totals = jnp.sum(weights, axis=1)
    partial_out = jnp.dot(weights.astype(jnp.bfloat16), value_rows, preferred_element_type=jnp.float32)
    block_max = jnp.where(active, block_max, NEG)
    totals = jnp.where(active, totals, 0.0)
    partial_out = jnp.where(active, partial_out, 0.0)
    return block_max, totals, partial_out


def combine(first_stats, second_stats):
    max_one, total_one, out_one = first_stats
    max_two, total_two, out_two = second_stats
    joint = jnp.maximum(max_one, max_two)
    scale_one = jnp.exp(max_one - joint)
    scale_two = jnp.exp(max_two - joint)
    return (joint, scale_one * total_one + scale_two * total_two,
            scale_one[..., None] * out_one + scale_two[..., None] * out_two)


def reference(queries, keys, values, group_mask, noise_level, token_count, level_gate):
    positions = jnp.arange(SEQ)
    head_numbers = jnp.arange(HEADS).astype(jnp.int32)
    results = []
    for target in range(GROUPS):
        earliest = max(0, target - WIN + 1)
        blocks = target + 1 - earliest
        query_heads = queries[target].reshape(SEQ, HEADS, HD).transpose(1, 0, 2)
        key_heads = keys[earliest:target + 1].reshape(blocks, SEQ, HEADS, HD).transpose(2, 0, 1, 3)
        value_heads = values[earliest:target + 1].reshape(blocks, SEQ, HEADS, HD).transpose(2, 0, 1, 3)

        def per_head(operands, target=target, earliest=earliest, blocks=blocks):
            head_number, query_rows, key_stack, value_stack = operands
            carried = (jnp.full((SEQ,), NEG, jnp.float32), jnp.zeros((SEQ,), jnp.float32),
                       jnp.zeros((SEQ, HD), jnp.float32))
            for offset in range(blocks):
                source = earliest + offset
                valid_keys = positions < token_count[source]
                active = group_mask[target, source, head_number] == 1
                carried = combine(carried, block_stats(query_rows, key_stack[offset], value_stack[offset], valid_keys, active))
            return carried[2] / carried[1][:, None]

        attended = lax.map(per_head, (head_numbers, query_heads, key_heads, value_heads))
        attended = attended.transpose(1, 0, 2).reshape(SEQ, HEADS * HD)
        results.append((attended * level_gate[noise_level[target]]).astype(jnp.bfloat16))
    return jnp.stack(results)
```

```python
import functools

import jax
import jax.numpy as jnp
from jax import lax
from jax.experimental import pallas as pl
from jax.experimental.pallas import tpu as pltpu
from jax.sharding import PartitionSpec as P

HD = 128
NEG = -1e30
SCALE = HD**-0.5 * 1.4426950408889634
LIMIT = 100.0
BF = jnp.bfloat16
F32 = jnp.float32
VMEM_LIMIT = 48 * 2**20


def params():
    return pltpu.CompilerParams(vmem_limit_bytes=VMEM_LIMIT)


def dot(a, b, ca, cb):
    return lax.dot_general(a, b, (((ca,), (cb,)), ((), ())), preferred_element_type=F32)


def split_kernel(flip_ref, k_ref, v_ref, q_ref, kv_out, q_out):
    flip = flip_ref[0]
    heads = k_ref.shape[1] // HD
    for h in range(heads):
        cols = slice(h * HD, (h + 1) * HD)
        place = h + flip * (1 - 2 * (h % 2))
        kv_out[place, 0] = k_ref[:, cols]
        kv_out[place, 1] = v_ref[:, cols].T
        q_out[place] = q_ref[:, cols]


def split_heads(flip, keys, values, queries):
    rows, width = keys.shape
    heads = width // HD
    per = 8
    spec = pl.BlockSpec((rows, per * HD), lambda i, f: (0, i))
    return pl.pallas_call(
        split_kernel,
        grid_spec=pltpu.PrefetchScalarGridSpec(
            num_scalar_prefetch=1,
            grid=(heads // per,),
            in_specs=[spec, spec, spec],
            out_specs=[
                pl.BlockSpec((per, 2, rows, HD), lambda i, f: (i, 0, 0, 0)),
                pl.BlockSpec((per, rows, HD), lambda i, f: (i, 0, 0)),
            ],
        ),
        out_shape=[
            jax.ShapeDtypeStruct((heads, 2, rows, HD), BF),
            jax.ShapeDtypeStruct((heads, rows, HD), BF),
        ],
        compiler_params=params(),
        name="split_heads",
    )(flip, keys, values, queries)


def merge_kernel(flip_ref, o_ref, out_ref):
    flip = flip_ref[0]
    for h in range(o_ref.shape[0]):
        place = h + flip * (1 - 2 * (h % 2))
        out_ref[:, h * HD : (h + 1) * HD] = o_ref[place]


def merge_heads(flip, blocks):
    heads, rows, _ = blocks.shape
    per = 8
    return pl.pallas_call(
        merge_kernel,
        grid_spec=pltpu.PrefetchScalarGridSpec(
            num_scalar_prefetch=1,
            grid=(heads // per,),
            in_specs=[pl.BlockSpec((per, rows, HD), lambda i, f: (i, 0, 0))],
            out_specs=pl.BlockSpec((rows, per * HD), lambda i, f: (0, i)),
        ),
        out_shape=jax.ShapeDtypeStruct((rows, heads * HD), BF),
        compiler_params=params(),
        name="merge_heads",
    )(flip, blocks)


def largest_norm(rows):
    squares = dot(rows * rows, jnp.ones((HD, HD), BF), 1, 0)
    return jnp.max(squares)


def key_block(kv_ref, first, blocks):
    return kv_ref[pl.ds(first, blocks), 0].reshape(blocks * HD, HD)


def value_block(kv_ref, first, blocks):
    return jnp.concatenate([kv_ref[first + b, 1] for b in range(blocks)], axis=1)


def pair_body(q, kv_ref, key_norm, live, m_ref, l_ref, acc_ref, first_pair):
    heads = kv_ref.shape[0]
    sure = heads // 2
    step = 4
    extra = pl.cdiv(live - sure * HD, step * HD)
    bounded = largest_norm(q) * key_norm * (SCALE * SCALE) <= LIMIT * LIMIT
    if first_pair:
        unshifted = bounded
        m_ref[...] = jnp.where(bounded, 0.0, NEG) * jnp.ones_like(m_ref)
        l_ref[...] = jnp.zeros_like(l_ref)
        acc_ref[...] = jnp.zeros_like(acc_ref)
    else:
        unshifted = jnp.logical_and(bounded, jnp.max(jnp.abs(m_ref[...])) == 0.0)

    def weights(first, blocks, masked):
        p = jnp.exp2(dot(key_block(kv_ref, first, blocks), q, 1, 1) * SCALE)
        if masked:
            rows = lax.broadcasted_iota(jnp.int32, (blocks * HD, 1), 0) + first * HD
            p = jnp.where(rows < live, p, 0.0)
        return p

    @pl.when(unshifted)
    def _():
        p = weights(0, sure, False)
        l_ref[...] += jnp.sum(p, axis=0, keepdims=True)
        acc_ref[...] += dot(value_block(kv_ref, 0, sure), p.astype(BF), 1, 0)

        @pl.loop(0, extra)
        def _(i):
            first = sure + i * step
            p = weights(first, step, True)
            l_ref[...] += jnp.sum(p, axis=0, keepdims=True)
            acc_ref[...] += dot(value_block(kv_ref, first, step), p.astype(BF), 1, 0)

    @pl.when(jnp.logical_not(unshifted))
    def _():
        @pl.loop(0, pl.cdiv(live, HD))
        def _(first):
            s = dot(key_block(kv_ref, first, 1), q, 1, 1) * SCALE
            rows = lax.broadcasted_iota(jnp.int32, (HD, 1), 0) + first * HD
            counted = rows < live
            s = jnp.where(counted, s, NEG)
            old = m_ref[...]
            new = jnp.maximum(old, jnp.max(s, axis=0, keepdims=True))
            p = jnp.where(counted, jnp.exp2(s - new), 0.0)
            shrink = jnp.exp2(old - new)
            m_ref[...] = new
            l_ref[...] = l_ref[...] * shrink + jnp.sum(p, axis=0, keepdims=True)
            acc_ref[...] = acc_ref[...] * shrink + dot(kv_ref[first, 1], p.astype(BF), 1, 0)


def first_kernel(info_ref, q_ref, kv_ref, acc_out, m_out, l_out, norm_ref):
    @pl.when(pl.program_id(0) == 0)
    def _():
        norm_ref[0] = largest_norm(kv_ref[:, 0].reshape(-1, HD))

    pair_body(q_ref[...], kv_ref, norm_ref[0], info_ref[1], m_out, l_out, acc_out, True)


def next_kernel(last, info_ref, *refs):
    if last:
        q_ref, kv_ref, gate_ref, acc_in, m_in, l_in, out_ref, norm_ref, acc, m, l = refs
    else:
        q_ref, kv_ref, acc_in, m_in, l_in, acc, m, l, norm_ref = refs

    active = info_ref[0] == 1
    acc[...] = acc_in[...]
    m[...] = m_in[...]
    l[...] = l_in[...]

    @pl.when(active)
    def _():
        @pl.when(pl.program_id(0) == 0)
        def _():
            norm_ref[0] = largest_norm(kv_ref[:, 0].reshape(-1, HD))

        pair_body(q_ref[...], kv_ref, norm_ref[0], info_ref[1], m, l, acc, False)

    if last:
        out_ref[...] = ((acc[...] / l[...]).T * gate_ref[...]).astype(BF)


BQ = 2048


def attend(info, q, kv, state=None, gate=None):
    seq = q.shape[0]
    last = gate is not None
    row_spec = pl.BlockSpec((BQ, HD), lambda i, s: (i, 0))
    kv_spec = pl.BlockSpec(kv.shape, lambda i, s: (0, 0, 0, 0))
    acc_spec = pl.BlockSpec((HD, BQ), lambda i, s: (0, i))
    one_spec = pl.BlockSpec((1, BQ), lambda i, s: (0, i))
    state_specs = [acc_spec, one_spec, one_spec]
    state_shapes = [
        jax.ShapeDtypeStruct((HD, seq), F32),
        jax.ShapeDtypeStruct((1, seq), F32),
        jax.ShapeDtypeStruct((1, seq), F32),
    ]
    scratch = [pltpu.SMEM((1,), F32)]
    in_specs = [row_spec, kv_spec]
    operands = [q, kv]
    out_specs, out_shape = state_specs, state_shapes
    if state is None:
        kernel = first_kernel
    else:
        kernel = functools.partial(next_kernel, last)
        if last:
            in_specs.append(pl.BlockSpec((1, HD), lambda i, s: (0, 0)))
            operands.append(gate)
            out_specs = row_spec
            out_shape = jax.ShapeDtypeStruct((seq, HD), BF)
            scratch += [pltpu.VMEM((HD, BQ), F32), pltpu.VMEM((1, BQ), F32), pltpu.VMEM((1, BQ), F32)]
        in_specs += state_specs
        operands += list(state)
    return pl.pallas_call(
        kernel,
        grid_spec=pltpu.PrefetchScalarGridSpec(
            num_scalar_prefetch=1,
            grid=(seq // BQ,),
            in_specs=in_specs,
            out_specs=out_specs,
            scratch_shapes=scratch,
        ),
        out_shape=out_shape,
        compiler_params=params(),
        cost_estimate=pl.CostEstimate(
            flops=4 * seq * seq * HD, bytes_accessed=8 * 2**20, transcendentals=seq * seq
        ),
        name="attend",
    )(info, *operands)


def hop(value, pairs):
    heads = lax.axis_size("head")
    table = []
    for source, target in pairs:
        across = int(source // 2 != target // 2)
        table += [(source * heads + h, target * heads + (h ^ across)) for h in range(heads)]
    return lax.ppermute(value, ("group", "head"), table)


def shards(queries, keys, values, group_mask, noise_level, token_count, level_gate):
    group = lax.axis_index("group")
    place = lax.axis_index("head")
    flip = (group // 2).astype(jnp.int32)
    head = place ^ flip
    kv, q = split_heads(flip[None], keys[0], values[0], queries[0])
    kv = lax.all_to_all(kv, "head", split_axis=0, concat_axis=0, tiled=True)
    q = lax.all_to_all(q, "head", split_axis=0, concat_axis=0, tiled=True)
    q = q.reshape(-1, HD)
    half = kv.shape[0] // 2
    low, high = kv[:half], kv[half:]
    one_low = hop(low, [(0, 1), (1, 2), (2, 3)])
    one_high = hop(high, [(0, 1), (2, 3)])
    far_high = hop(high, [(1, 3)])
    swapped = hop(jnp.where(group == 2, one_low, far_high), [(2, 3), (3, 2)])
    one_back = jnp.concatenate([one_low, jnp.where(group == 2, swapped, one_high)])
    kv_late, _ = lax.optimization_barrier((kv, far_high))
    two_back = hop(kv_late, [(0, 2)])
    two_back = jnp.where(group == 3, jnp.concatenate([swapped, far_high]), two_back)

    def info(offset):
        source = jnp.maximum(group - offset, 0)
        active = (group >= offset) & (group_mask[group, source, head] == 1)
        return jnp.stack([active.astype(jnp.int32), token_count[source]])

    gate = lax.dynamic_slice(level_gate, (noise_level[group], head * HD), (1, HD))
    state = attend(info(0), q, kv)
    state = attend(info(1), q, one_back, state)
    out = attend(info(2), q, two_back, state, gate)
    out = out.reshape(kv.shape[0], -1, HD)
    out = lax.all_to_all(out, "head", split_axis=0, concat_axis=0, tiled=True)
    return merge_heads(flip[None], out)[None]


def solution(mesh):
    rows = P("group", "head", None)
    return jax.shard_map(
        shards,
        mesh=mesh,
        in_specs=(rows, rows, rows, P(), P(), P(), P()),
        out_specs=rows,
        check_vma=False,
    )
```

```python
import jax
import jax.numpy as jnp
from jax import lax
from jax.experimental import pallas as pl
from jax.experimental.pallas import tpu as pltpu
from jax.sharding import PartitionSpec as P

HD = 128
NEG = -1e30
SCALE = HD**-0.5 * 1.4426950408889634
LIMIT = 100.0
BF = jnp.bfloat16
F32 = jnp.float32
VMEM_LIMIT = 60 * 2**20


def params():
    return pltpu.CompilerParams(vmem_limit_bytes=VMEM_LIMIT)


def dot(a, b, ca, cb):
    return lax.dot_general(a, b, (((ca,), (cb,)), ((), ())), preferred_element_type=F32)


def head_block(h):
    return h + (lax.axis_index("group") // 2) * (1 - 2 * (h % 2))


def head_here():
    return head_block(lax.axis_index("head"))


def split_kernel(*refs):
    rows_refs, out_ref = refs[:-1], refs[-1]
    rows, width = rows_refs[0].shape
    for h in range(width // HD):
        for n, ref in enumerate(rows_refs):
            out_ref[head_block(h), n * rows : (n + 1) * rows] = ref[:, h * HD : (h + 1) * HD]


def split_heads(*arrays):
    rows, width = arrays[0].shape
    heads, per = width // HD, 8
    deep = rows * len(arrays)
    return pl.pallas_call(
        split_kernel,
        grid=(heads // per,),
        in_specs=[pl.BlockSpec((rows, per * HD), lambda i: (0, i))] * len(arrays),
        out_specs=pl.BlockSpec((per, deep, HD), lambda i: (i, 0, 0)),
        out_shape=jax.ShapeDtypeStruct((heads, deep, HD), BF),
        compiler_params=params(),
        name="split_heads",
    )(*arrays)


def merge_kernel(blocks_ref, out_ref):
    for h in range(blocks_ref.shape[0]):
        out_ref[:, h * HD : (h + 1) * HD] = blocks_ref[head_block(h)]


def merge_heads(blocks):
    heads, rows, _ = blocks.shape
    per = 8
    return pl.pallas_call(
        merge_kernel,
        grid=(heads // per,),
        in_specs=[pl.BlockSpec((per, rows, HD), lambda i: (i, 0, 0))],
        out_specs=pl.BlockSpec((rows, per * HD), lambda i: (0, i)),
        out_shape=jax.ShapeDtypeStruct((rows, heads * HD), BF),
        compiler_params=params(),
        name="merge_heads",
    )(blocks)


def largest_norm(rows):
    squares = dot(rows * rows, jnp.ones((HD, HD), BF), 1, 0)
    return jnp.max(squares)


def key_block(kv_ref, first, blocks):
    return kv_ref[pl.ds(first, blocks), :HD].reshape(blocks * HD, HD)


def value_block(kv_ref, first, blocks):
    return kv_ref[pl.ds(first, blocks), HD:].reshape(blocks * HD, HD)


STEP = 4


def pair_body(q, kv_ref, key_norm, live, m_ref, l_ref, acc_ref, first_pair):
    heads = kv_ref.shape[0]
    sure = heads // 2
    bounded = largest_norm(q) * key_norm * (SCALE * SCALE) <= LIMIT * LIMIT
    if first_pair:
        unshifted = bounded
        m_ref[...] = jnp.where(bounded, 0.0, NEG) * jnp.ones_like(m_ref)
        l_ref[...] = jnp.zeros_like(l_ref)
        acc_ref[...] = jnp.zeros_like(acc_ref)
    else:
        unshifted = jnp.logical_and(bounded, jnp.max(jnp.abs(m_ref[...])) == 0.0)

    def add(first, blocks, masked):
        p = jnp.exp2(dot(key_block(kv_ref, first, blocks), q, 1, 1) * SCALE)
        if masked:
            rows = lax.broadcasted_iota(jnp.int32, (blocks * HD, 1), 0) + first * HD
            p = jnp.where(rows < live, p, 0.0)
        l_ref[...] += jnp.sum(p, axis=0, keepdims=True)
        acc_ref[...] += dot(value_block(kv_ref, first, blocks), p.astype(BF), 0, 0)

    @pl.when(unshifted)
    def _():
        add(0, sure, False)
        extra = pl.cdiv(live - sure * HD, STEP * HD)
        for count in range(1, (heads - sure) // STEP + 1):

            @pl.when(extra == count)
            def _():
                add(sure, count * STEP, True)

    @pl.when(jnp.logical_not(unshifted))
    def _():
        @pl.loop(0, pl.cdiv(live, HD))
        def _(first):
            s = dot(key_block(kv_ref, first, 1), q, 1, 1) * SCALE
            rows = lax.broadcasted_iota(jnp.int32, (HD, 1), 0) + first * HD
            counted = rows < live
            s = jnp.where(counted, s, NEG)
            old = m_ref[...]
            new = jnp.maximum(old, jnp.max(s, axis=0, keepdims=True))
            p = jnp.where(counted, jnp.exp2(s - new), 0.0)
            shrink = jnp.exp2(old - new)
            m_ref[...] = new
            l_ref[...] = l_ref[...] * shrink + jnp.sum(p, axis=0, keepdims=True)
            acc_ref[...] = acc_ref[...] * shrink + dot(value_block(kv_ref, first, 1), p.astype(BF), 0, 0)


def set_key_norm(norm_ref, kv_ref):
    norm_ref[0] = largest_norm(key_block(kv_ref, 0, kv_ref.shape[0]))


def own_kernel(count_ref, q_ref, kv_ref, acc_ref, m_ref, l_ref, norm_ref):
    @pl.when(pl.program_id(0) == 0)
    def _():
        set_key_norm(norm_ref, kv_ref)

    live = count_ref[lax.axis_index("group")]
    pair_body(q_ref[...], kv_ref, norm_ref[0], live, m_ref, l_ref, acc_ref, True)


def source_of(mask_ref, offset):
    group = lax.axis_index("group")
    source = jnp.maximum(group - offset, 0)
    return source, jnp.logical_and(group >= offset, mask_ref[group, source, head_here()] == 1)


def one_kernel(count_ref, mask_ref, q_ref, kv_ref, acc_in, m_in, l_in, acc_ref, m_ref, l_ref, norm_ref):
    source, active = source_of(mask_ref, 1)
    acc_ref[...] = acc_in[...]
    m_ref[...] = m_in[...]
    l_ref[...] = l_in[...]

    @pl.when(active)
    def _():
        @pl.when(pl.program_id(0) == 0)
        def _():
            set_key_norm(norm_ref, kv_ref)

        pair_body(q_ref[...], kv_ref, norm_ref[0], count_ref[source], m_ref, l_ref, acc_ref, False)


def two_kernel(
    count_ref, mask_ref, level_ref, q_ref, near_ref, far_ref, gate_ref, acc_in, m_in, l_in,
    out_ref, kv_ref, sem, norm_ref, acc_ref, m_ref, l_ref,
):
    source, active = source_of(mask_ref, 2)
    group = lax.axis_index("group")
    acc_ref[...] = acc_in[...]
    m_ref[...] = m_in[...]
    l_ref[...] = l_in[...]

    @pl.when(active)
    def _():
        @pl.when(pl.program_id(0) == 0)
        def _():
            @pl.when(group == 3)
            def _():
                pltpu.make_async_copy(near_ref, kv_ref, sem).start()

            @pl.when(group != 3)
            def _():
                pltpu.make_async_copy(far_ref, kv_ref, sem).start()

            pltpu.make_async_copy(far_ref, kv_ref, sem).wait()
            set_key_norm(norm_ref, kv_ref)

        pair_body(q_ref[...], kv_ref, norm_ref[0], count_ref[source], m_ref, l_ref, acc_ref, False)

    column = pl.multiple_of(head_here() * HD, HD)
    gates = gate_ref[:, pl.ds(column, HD)]
    levels = lax.broadcasted_iota(jnp.int32, gates.shape, 0)
    gate = jnp.sum(jnp.where(levels == level_ref[group], gates, 0.0), axis=0, keepdims=True)
    out_ref[...] = ((acc_ref[...] / l_ref[...]).T * gate).astype(BF)


BQ = 2048


def call(kernel, scalars, operands, in_specs, out_specs, out_shape, scratch, seq, name):
    return pl.pallas_call(
        kernel,
        grid_spec=pltpu.PrefetchScalarGridSpec(
            num_scalar_prefetch=len(scalars),
            grid=(seq // BQ,),
            in_specs=in_specs,
            out_specs=out_specs,
            scratch_shapes=scratch,
        ),
        out_shape=out_shape,
        compiler_params=params(),
        cost_estimate=pl.CostEstimate(
            flops=4 * seq * seq * HD, bytes_accessed=8 * 2**20, transcendentals=seq * seq
        ),
        name=name,
    )(*scalars, *operands)


def attend(q, own, one, far, group_mask, noise_level, token_count, level_gate):
    seq = q.shape[0]
    rows = pl.BlockSpec((BQ, HD), lambda i, *s: (i, 0))
    kv = pl.BlockSpec(own.shape, lambda i, *s: (0, 0, 0))
    state = [
        pl.BlockSpec((HD, BQ), lambda i, *s: (0, i)),
        pl.BlockSpec((1, BQ), lambda i, *s: (0, i)),
        pl.BlockSpec((1, BQ), lambda i, *s: (0, i)),
    ]
    state_shape = [
        jax.ShapeDtypeStruct((HD, seq), F32),
        jax.ShapeDtypeStruct((1, seq), F32),
        jax.ShapeDtypeStruct((1, seq), F32),
    ]
    norm = pltpu.SMEM((1,), F32)
    carried = call(
        own_kernel, [token_count], [q, own], [rows, kv], state, state_shape, [norm], seq, "own_group"
    )
    one, carried = lax.optimization_barrier((one, carried))
    near = hop(one, [(2, 3)])
    carried = call(
        one_kernel, [token_count, group_mask], [q, one, *carried], [rows, kv, *state], state,
        state_shape, [norm], seq, "one_back",
    )
    whole = pl.BlockSpec(level_gate.shape, lambda i, *s: (0, 0))
    anywhere = pl.BlockSpec(memory_space=pl.ANY)
    scratch = [
        pltpu.VMEM(own.shape, BF),
        pltpu.SemaphoreType.DMA,
        norm,
        pltpu.VMEM((HD, BQ), F32),
        pltpu.VMEM((1, BQ), F32),
        pltpu.VMEM((1, BQ), F32),
    ]
    return call(
        two_kernel, [token_count, group_mask, noise_level],
        [q, near, far, level_gate, *carried], [rows, anywhere, anywhere, whole, *state],
        rows, jax.ShapeDtypeStruct((seq, HD), BF), scratch, seq, "two_back",
    )


def hop(value, pairs):
    heads = lax.axis_size("head")
    table = []
    for source, target in pairs:
        across = int(source // 2 != target // 2)
        table += [(source * heads + h, target * heads + (h ^ across)) for h in range(heads)]
    return lax.ppermute(value, ("group", "head"), table)


def exchange(blocks):
    return lax.all_to_all(blocks, "head", split_axis=0, concat_axis=0, tiled=True)


def shards(queries, keys, values, group_mask, noise_level, token_count, level_gate):
    kv = split_heads(keys[0], values[0])
    query_rows, kv = lax.optimization_barrier((queries[0], kv))
    q = split_heads(query_rows)
    kv = exchange(kv)
    q, kv = lax.optimization_barrier((q, kv))
    q = exchange(q).reshape(-1, HD)
    one = hop(kv, [(0, 1), (1, 2), (2, 3)])
    late, q = lax.optimization_barrier((kv, q))
    far = hop(late, [(0, 2)])
    out = attend(q, kv, one, far, group_mask, noise_level, token_count, level_gate)
    return merge_heads(exchange(out.reshape(kv.shape[0], -1, HD)))[None]


def solution(mesh):
    rows = P("group", "head", None)
    return jax.shard_map(
        shards,
        mesh=mesh,
        in_specs=(rows, rows, rows, P(), P(), P(), P()),
        out_specs=rows,
        check_vma=False,
    )
```

```python
import jax
import jax.numpy as jnp
from jax import lax
from jax.experimental import pallas as pl
from jax.experimental.pallas import tpu as pltpu
from jax.sharding import PartitionSpec as P

HD = 128
NEG = -1e30
SCALE = HD**-0.5 * 1.4426950408889634
LEAST, MOST = 2.0**-80, 2.0**100
BF = jnp.bfloat16
F32 = jnp.float32
VMEM_LIMIT = 40 * 2**20


def params():
    return pltpu.CompilerParams(vmem_limit_bytes=VMEM_LIMIT)


def dot(a, b, ca, cb):
    return lax.dot_general(a, b, (((ca,), (cb,)), ((), ())), preferred_element_type=F32)


def head_block(h):
    return h + (lax.axis_index("group") // 2) * (1 - 2 * (h % 2))


def head_here():
    return head_block(lax.axis_index("head"))


PER = 8
VMEM = pl.BlockSpec(memory_space=pltpu.VMEM)


def split_kernel(*refs):
    rows_refs, out_ref = refs[:-1], refs[-1]
    rows, width = rows_refs[0].shape
    first = pl.program_id(0) * PER
    for h in range(PER):
        for n, ref in enumerate(rows_refs):
            out_ref[first + head_block(h), n * rows : (n + 1) * rows] = ref[:, h * HD : (h + 1) * HD]


def split_heads(*arrays):
    rows, width = arrays[0].shape
    heads = width // HD
    deep = rows * len(arrays)
    return pl.pallas_call(
        split_kernel,
        grid=(heads // PER,),
        in_specs=[pl.BlockSpec((rows, PER * HD), lambda i: (0, i))] * len(arrays),
        out_specs=VMEM,
        out_shape=jax.ShapeDtypeStruct((heads, deep, HD), BF),
        compiler_params=params(),
        name="split_heads",
    )(*arrays)


def merge_kernel(blocks_ref, out_ref):
    first = pl.program_id(0) * PER
    for h in range(PER):
        out_ref[:, h * HD : (h + 1) * HD] = blocks_ref[first + head_block(h)]


def merge_heads(blocks):
    heads, rows, _ = blocks.shape
    return pl.pallas_call(
        merge_kernel,
        grid=(heads // PER,),
        in_specs=[VMEM],
        out_specs=pl.BlockSpec((rows, PER * HD), lambda i: (0, i)),
        out_shape=jax.ShapeDtypeStruct((rows, heads * HD), BF),
        compiler_params=params(),
        name="merge_heads",
    )(blocks)


BQ = 2048
STEP = 4
CHUNK = 8


def key_block(kv_ref, first, blocks):
    return kv_ref[pl.ds(first, blocks), :HD].reshape(blocks * HD, HD)


def value_block(kv_ref, first, blocks):
    return kv_ref[pl.ds(first, blocks), HD:].reshape(blocks * HD, HD)


def unshifted_sums(q, kv_ref, live, blocks, l_ref, acc_ref, l_old, acc_old):
    pieces = [(f, min(CHUNK, blocks - STEP - f), False) for f in range(0, blocks - STEP, CHUNK)]
    for n, (first, count, masked) in enumerate(pieces + [(blocks - STEP, STEP, True)]):
        p = jnp.exp2(dot(key_block(kv_ref, first, count), q, 1, 1) * SCALE)
        if masked:
            rows = lax.broadcasted_iota(jnp.int32, (count * HD, 1), 0) + first * HD
            p = jnp.where(rows < live, p, 0.0)
        l_here = jnp.sum(p, axis=0, keepdims=True)
        acc_here = dot(value_block(kv_ref, first, count), p.astype(BF), 0, 0)
        if n > 0:
            l_here, acc_here = l_ref[...] + l_here, acc_ref[...] + acc_here
        elif l_old is not None:
            l_here, acc_here = l_old[...] + l_here, acc_old[...] + acc_here
        l_ref[...] = l_here
        acc_ref[...] = acc_here


def shifted_sums(q, kv_ref, live, m_ref, l_ref, acc_ref):
    @pl.loop(0, pl.cdiv(live, HD))
    def _(first):
        s = dot(key_block(kv_ref, first, 1), q, 1, 1) * SCALE
        rows = lax.broadcasted_iota(jnp.int32, (HD, 1), 0) + first * HD
        counted = rows < live
        s = jnp.where(counted, s, NEG)
        old = m_ref[...]
        new = jnp.maximum(old, jnp.max(s, axis=0, keepdims=True))
        p = jnp.where(counted, jnp.exp2(s - new), 0.0)
        shrink = jnp.exp2(old - new)
        m_ref[...] = new
        l_ref[...] = l_ref[...] * shrink + jnp.sum(p, axis=0, keepdims=True)
        acc_ref[...] = acc_ref[...] * shrink + dot(value_block(kv_ref, first, 1), p.astype(BF), 0, 0)


def pair_sums(q, kv_ref, live, old, new):
    m_ref, l_ref, acc_ref = new
    heads = kv_ref.shape[0]
    need = jnp.maximum(pl.cdiv(live, STEP * HD), heads // (2 * STEP) + 1)
    for count in range(heads // (2 * STEP) + 1, heads // STEP + 1):

        @pl.when(need == count)
        def _():
            _, l_old, acc_old = old or (None, None, None)
            unshifted_sums(q, kv_ref, live, count * STEP, l_ref, acc_ref, l_old, acc_old)

    m_ref[...] = jnp.zeros_like(m_ref) if old is None else old[0][...]
    sums = l_ref[...]
    good = jnp.logical_and(jnp.min(sums) >= LEAST, jnp.max(sums) <= MOST)
    if old is not None:
        good = jnp.logical_and(good, jnp.max(jnp.abs(old[0][...])) == 0.0)

    @pl.when(jnp.logical_not(good))
    def _():
        if old is None:
            m_ref[...] = jnp.full_like(m_ref, NEG)
            l_ref[...] = jnp.zeros_like(l_ref)
            acc_ref[...] = jnp.zeros_like(acc_ref)
        else:
            l_ref[...] = old[1][...]
            acc_ref[...] = old[2][...]
        shifted_sums(q, kv_ref, live, m_ref, l_ref, acc_ref)


def tile(state, i):
    columns = pl.ds(pl.multiple_of(i * BQ, BQ), BQ)
    return tuple(ref.at[:, columns] for ref in state)


def own_kernel(count_ref, q_ref, kv_ref, m_ref, l_ref, acc_ref):
    live = count_ref[lax.axis_index("group")]

    @pl.loop(0, q_ref.shape[0] // BQ)
    def _(i):
        q = q_ref[pl.ds(pl.multiple_of(i * BQ, BQ), BQ), :]
        pair_sums(q, kv_ref, live, None, tile((m_ref, l_ref, acc_ref), i))


def source_of(mask_ref, offset):
    group = lax.axis_index("group")
    source = jnp.maximum(group - offset, 0)
    return source, jnp.logical_and(group >= offset, mask_ref[group, source, head_here()] == 1)


def one_kernel(count_ref, mask_ref, q_ref, kv_ref, m_in, l_in, acc_in, m_ref, l_ref, acc_ref):
    source, active = source_of(mask_ref, 1)
    old, new = (m_in, l_in, acc_in), (m_ref, l_ref, acc_ref)

    @pl.when(active)
    def _():
        @pl.loop(0, q_ref.shape[0] // BQ)
        def _(i):
            q = q_ref[pl.ds(pl.multiple_of(i * BQ, BQ), BQ), :]
            pair_sums(q, kv_ref, count_ref[source], tile(old, i), tile(new, i))

    @pl.when(jnp.logical_not(active))
    def _():
        for old_ref, new_ref in zip(old, new):
            new_ref[...] = old_ref[...]


def two_kernel(
    count_ref, mask_ref, level_ref, q_ref, near_ref, far_ref, gate_ref, m_in, l_in, acc_in,
    out_ref, kv_ref, sems, m_ref, l_ref, acc_ref,
):
    source, active = source_of(mask_ref, 2)
    group = lax.axis_index("group")
    i = pl.program_id(0)
    new = (m_ref, l_ref, acc_ref)
    pieces = sems.shape[0]
    deep = kv_ref.shape[0] // pieces

    def copy(ref, n):
        part = pl.ds(n * deep, deep)
        return pltpu.make_async_copy(ref.at[part], kv_ref.at[part], sems.at[n])

    @pl.when(active)
    def _():
        @pl.when(i == 0)
        def _():
            @pl.when(group == 3)
            def _():
                for n in range(pieces):
                    copy(near_ref, n).start()

            @pl.when(group != 3)
            def _():
                for n in range(pieces):
                    copy(far_ref, n).start()

            for n in range(pieces):
                copy(far_ref, n).wait()

        q = q_ref[pl.ds(pl.multiple_of(i * BQ, BQ), BQ), :]
        pair_sums(q, kv_ref, count_ref[source], tile((m_in, l_in, acc_in), i), new)

    @pl.when(jnp.logical_not(active))
    def _():
        for old_ref, new_ref in zip(tile((m_in, l_in, acc_in), i), new):
            new_ref[...] = old_ref[...]

    gates = gate_ref[:, pl.ds(pl.multiple_of(head_here() * HD, HD), HD)]
    levels = lax.broadcasted_iota(jnp.int32, gates.shape, 0)
    gate = jnp.sum(jnp.where(levels == level_ref[group], gates, 0.0), axis=0, keepdims=True)
    out_ref[...] = ((acc_ref[...] / l_ref[...]).T * gate).astype(BF)


def call(kernel, scalars, operands, in_specs, out_specs, out_shape, name, grid=(1,), scratch=()):
    seq = operands[0].shape[0]
    return pl.pallas_call(
        kernel,
        grid_spec=pltpu.PrefetchScalarGridSpec(
            num_scalar_prefetch=len(scalars),
            grid=grid,
            in_specs=in_specs,
            out_specs=out_specs,
            scratch_shapes=scratch,
        ),
        out_shape=out_shape,
        compiler_params=params(),
        cost_estimate=pl.CostEstimate(
            flops=4 * seq * seq * HD, bytes_accessed=8 * 2**20, transcendentals=seq * seq
        ),
        name=name,
    )(*scalars, *operands)


def attend(q, own, one, far, group_mask, noise_level, token_count, level_gate):
    seq = q.shape[0]
    shapes = [jax.ShapeDtypeStruct((n, seq), F32) for n in (1, 1, HD)]
    carried = call(own_kernel, [token_count], [q, own], [VMEM] * 2, [VMEM] * 3, shapes, "own_group")
    one, carried = lax.optimization_barrier((one, carried))
    near = hop(one, [(2, 3)])
    carried = call(
        one_kernel, [token_count, group_mask], [q, one, *carried], [VMEM] * 5, [VMEM] * 3, shapes,
        "one_back",
    )
    anywhere = pl.BlockSpec(memory_space=pl.ANY)
    scratch = [
        pltpu.VMEM(own.shape, BF),
        pltpu.SemaphoreType.DMA((8,)),
        pltpu.VMEM((1, BQ), F32),
        pltpu.VMEM((1, BQ), F32),
        pltpu.VMEM((HD, BQ), F32),
    ]
    return call(
        two_kernel, [token_count, group_mask, noise_level], [q, near, far, level_gate, *carried],
        [VMEM, anywhere, anywhere, VMEM, VMEM, VMEM, VMEM],
        pl.BlockSpec((BQ, HD), lambda i, *s: (i, 0)), jax.ShapeDtypeStruct((seq, HD), BF),
        "two_back", (seq // BQ,), scratch,
    )


def hop(value, pairs):
    heads = lax.axis_size("head")
    table = []
    for source, target in pairs:
        across = int(source // 2 != target // 2)
        table += [(source * heads + h, target * heads + (h ^ across)) for h in range(heads)]
    return lax.ppermute(value, ("group", "head"), table)


def exchange(blocks):
    return lax.all_to_all(blocks, "head", split_axis=0, concat_axis=0, tiled=True)


def shards(queries, keys, values, group_mask, noise_level, token_count, level_gate):
    kv = split_heads(keys[0], values[0])
    query_rows, kv = lax.optimization_barrier((queries[0], kv))
    q = split_heads(query_rows)
    kv = exchange(kv)
    q, kv = lax.optimization_barrier((q, kv))
    q = exchange(q).reshape(-1, HD)
    one = hop(kv, [(0, 1), (1, 2), (2, 3)])
    late, q = lax.optimization_barrier((kv, q))
    far = hop(late, [(0, 2)])
    out = attend(q, kv, one, far, group_mask, noise_level, token_count, level_gate)
    return merge_heads(exchange(out.reshape(kv.shape[0], -1, HD)))[None]


def solution(mesh):
    rows = P("group", "head", None)
    return jax.shard_map(
        shards,
        mesh=mesh,
        in_specs=(rows, rows, rows, P(), P(), P(), P()),
        out_specs=rows,
        check_vma=False,
    )
```

```python
import jax
import jax.numpy as jnp
from jax import lax
from jax.experimental import pallas as pl
from jax.experimental.pallas import tpu as pltpu
from jax.sharding import PartitionSpec as P

HD = 128
NEG = -1e30
SCALE = HD**-0.5 * 1.4426950408889634
LEAST, MOST = 2.0**-80, 2.0**100
BF = jnp.bfloat16
F32 = jnp.float32
VMEM_LIMIT = 40 * 2**20


def params():
    return pltpu.CompilerParams(vmem_limit_bytes=VMEM_LIMIT)


def dot(a, b, ca, cb):
    return lax.dot_general(a, b, (((ca,), (cb,)), ((), ())), preferred_element_type=F32)


def head_block(h):
    return h + (lax.axis_index("group") // 2) * (1 - 2 * (h % 2))


def head_here():
    return head_block(lax.axis_index("head"))


PER = 8
VMEM = pl.BlockSpec(memory_space=pltpu.VMEM)


def split_kernel(*refs):
    rows_refs, out_ref = refs[:-1], refs[-1]
    rows, width = rows_refs[0].shape
    first = pl.program_id(0) * PER
    for h in range(PER):
        for n, ref in enumerate(rows_refs):
            out_ref[first + head_block(h), n * rows : (n + 1) * rows] = ref[:, h * HD : (h + 1) * HD]


def split_heads(*arrays):
    rows, width = arrays[0].shape
    heads = width // HD
    deep = rows * len(arrays)
    return pl.pallas_call(
        split_kernel,
        grid=(heads // PER,),
        in_specs=[pl.BlockSpec((rows, PER * HD), lambda i: (0, i))] * len(arrays),
        out_specs=VMEM,
        out_shape=jax.ShapeDtypeStruct((heads, deep, HD), BF),
        compiler_params=params(),
        name="split_heads",
    )(*arrays)


def merge_kernel(blocks_ref, out_ref):
    first = pl.program_id(0) * PER
    for h in range(PER):
        out_ref[:, h * HD : (h + 1) * HD] = blocks_ref[first + head_block(h)]


def merge_heads(blocks):
    heads, rows, _ = blocks.shape
    return pl.pallas_call(
        merge_kernel,
        grid=(heads // PER,),
        in_specs=[VMEM],
        out_specs=pl.BlockSpec((rows, PER * HD), lambda i: (0, i)),
        out_shape=jax.ShapeDtypeStruct((rows, heads * HD), BF),
        compiler_params=params(),
        name="merge_heads",
    )(blocks)


BQ = 2048
STEP = 4


def key_block(kv_ref, first, blocks):
    return kv_ref[pl.ds(first, blocks), :HD].reshape(blocks * HD, HD)


def value_block(kv_ref, first, blocks):
    return kv_ref[pl.ds(first, blocks), HD:].reshape(blocks * HD, HD)


def unshifted_sums(q, kv_ref, live, first, blocks, masked, l_ref, acc_ref, l_old, acc_old):
    p = jnp.exp2(dot(key_block(kv_ref, first, blocks), q, 1, 1) * SCALE)
    if masked:
        rows = lax.broadcasted_iota(jnp.int32, (blocks * HD, 1), 0) + first * HD
        p = jnp.where(rows < live, p, 0.0)
    l_here = jnp.sum(p, axis=0, keepdims=True)
    acc_here = dot(value_block(kv_ref, first, blocks), p.astype(BF), 0, 0)
    l_ref[...] = l_here if l_old is None else l_old[...] + l_here
    acc_ref[...] = acc_here if acc_old is None else acc_old[...] + acc_here


def shifted_sums(q, kv_ref, live, m_ref, l_ref, acc_ref):
    @pl.loop(0, pl.cdiv(live, HD))
    def _(first):
        s = dot(key_block(kv_ref, first, 1), q, 1, 1) * SCALE
        rows = lax.broadcasted_iota(jnp.int32, (HD, 1), 0) + first * HD
        counted = rows < live
        s = jnp.where(counted, s, NEG)
        old = m_ref[...]
        new = jnp.maximum(old, jnp.max(s, axis=0, keepdims=True))
        p = jnp.where(counted, jnp.exp2(s - new), 0.0)
        shrink = jnp.exp2(old - new)
        m_ref[...] = new
        l_ref[...] = l_ref[...] * shrink + jnp.sum(p, axis=0, keepdims=True)
        acc_ref[...] = acc_ref[...] * shrink + dot(value_block(kv_ref, first, 1), p.astype(BF), 0, 0)


def pair_sums(q, kv_ref, live, old, new):
    m_ref, l_ref, acc_ref = new
    sure = kv_ref.shape[0] // 2
    _, l_old, acc_old = old or (None, None, None)
    unshifted_sums(q, kv_ref, live, 0, sure, False, l_ref, acc_ref, l_old, acc_old)
    steps = pl.cdiv(live - sure * HD, STEP * HD)
    pairs = steps // 2

    @pl.loop(0, pairs)
    def _(n):
        first = sure + n * 2 * STEP
        unshifted_sums(q, kv_ref, live, first, 2 * STEP, True, l_ref, acc_ref, l_ref, acc_ref)

    @pl.when(steps % 2 == 1)
    def _():
        first = sure + pairs * 2 * STEP
        unshifted_sums(q, kv_ref, live, first, STEP, True, l_ref, acc_ref, l_ref, acc_ref)

    m_ref[...] = jnp.zeros_like(m_ref) if old is None else old[0][...]
    sums = l_ref[...]
    good = jnp.logical_and(jnp.min(sums) >= LEAST, jnp.max(sums) <= MOST)
    if old is not None:
        good = jnp.logical_and(good, jnp.max(jnp.abs(old[0][...])) == 0.0)

    @pl.when(jnp.logical_not(good))
    def _():
        if old is None:
            m_ref[...] = jnp.full_like(m_ref, NEG)
            l_ref[...] = jnp.zeros_like(l_ref)
            acc_ref[...] = jnp.zeros_like(acc_ref)
        else:
            l_ref[...] = old[1][...]
            acc_ref[...] = old[2][...]
        shifted_sums(q, kv_ref, live, m_ref, l_ref, acc_ref)


DEEP = HD + 8


def parts(ref):
    return ref.at[HD : HD + 1], ref.at[HD + 1 : HD + 2], ref.at[:HD]


def tile(ref, i):
    return ref.at[:, pl.ds(pl.multiple_of(i * BQ, BQ), BQ)]


def query_tile(q_ref, i):
    return q_ref[pl.ds(pl.multiple_of(i * BQ, BQ), BQ), :]


def own_kernel(count_ref, q_ref, kv_ref, new_ref):
    live = count_ref[lax.axis_index("group")]

    @pl.loop(0, q_ref.shape[0] // BQ)
    def _(i):
        pair_sums(query_tile(q_ref, i), kv_ref, live, None, parts(tile(new_ref, i)))


def source_of(mask_ref, offset):
    group = lax.axis_index("group")
    source = jnp.maximum(group - offset, 0)
    return source, jnp.logical_and(group >= offset, mask_ref[group, source, head_here()] == 1)


def one_kernel(count_ref, mask_ref, q_ref, kv_ref, old_ref, new_ref):
    source, active = source_of(mask_ref, 1)

    @pl.loop(0, q_ref.shape[0] // BQ)
    def _(i):
        old, new = tile(old_ref, i), tile(new_ref, i)

        @pl.when(active)
        def _():
            pair_sums(query_tile(q_ref, i), kv_ref, count_ref[source], parts(old), parts(new))

        @pl.when(jnp.logical_not(active))
        def _():
            new[...] = old[...]


def two_kernel(
    count_ref, mask_ref, level_ref, q_ref, near_ref, far_ref, gate_ref, old_ref,
    out_ref, kv_ref, sems, new_ref,
):
    source, active = source_of(mask_ref, 2)
    group = lax.axis_index("group")
    i = pl.program_id(0)
    old = tile(old_ref, i)
    pieces = sems.shape[0]
    deep = kv_ref.shape[0] // pieces

    def copy(ref, n):
        part = pl.ds(n * deep, deep)
        return pltpu.make_async_copy(ref.at[part], kv_ref.at[part], sems.at[n])

    @pl.when(active)
    def _():
        @pl.when(i == 0)
        def _():
            @pl.when(group == 3)
            def _():
                for n in range(pieces):
                    copy(near_ref, n).start()

            @pl.when(group != 3)
            def _():
                for n in range(pieces):
                    copy(far_ref, n).start()

            for n in range(pieces):
                copy(far_ref, n).wait()

        pair_sums(query_tile(q_ref, i), kv_ref, count_ref[source], parts(old), parts(new_ref))

    @pl.when(jnp.logical_not(active))
    def _():
        new_ref[...] = old[...]

    gates = gate_ref[:, pl.ds(pl.multiple_of(head_here() * HD, HD), HD)]
    levels = lax.broadcasted_iota(jnp.int32, gates.shape, 0)
    gate = jnp.sum(jnp.where(levels == level_ref[group], gates, 0.0), axis=0, keepdims=True)
    _, l_ref, acc_ref = parts(new_ref)
    out_ref[...] = ((acc_ref[...] / l_ref[...]).T * gate).astype(BF)


def call(kernel, scalars, operands, in_specs, out_specs, out_shape, name, grid=(1,), scratch=()):
    seq = operands[0].shape[0]
    return pl.pallas_call(
        kernel,
        grid_spec=pltpu.PrefetchScalarGridSpec(
            num_scalar_prefetch=len(scalars),
            grid=grid,
            in_specs=in_specs,
            out_specs=out_specs,
            scratch_shapes=scratch,
        ),
        out_shape=out_shape,
        compiler_params=params(),
        cost_estimate=pl.CostEstimate(
            flops=4 * seq * seq * HD, bytes_accessed=8 * 2**20, transcendentals=seq * seq
        ),
        name=name,
    )(*scalars, *operands)


def attend(q, own, one, far, group_mask, noise_level, token_count, level_gate):
    seq = q.shape[0]
    state = jax.ShapeDtypeStruct((DEEP, seq), F32)
    carried = call(own_kernel, [token_count], [q, own], [VMEM] * 2, VMEM, state, "own_group")
    one, carried = lax.optimization_barrier((one, carried))
    near = hop(one, [(2, 3)])
    carried = call(
        one_kernel, [token_count, group_mask], [q, one, carried], [VMEM] * 3, VMEM, state, "one_back"
    )
    anywhere = pl.BlockSpec(memory_space=pl.ANY)
    scratch = [
        pltpu.VMEM(own.shape, BF),
        pltpu.SemaphoreType.DMA((8,)),
        pltpu.VMEM((DEEP, BQ), F32),
    ]
    return call(
        two_kernel, [token_count, group_mask, noise_level], [q, near, far, level_gate, carried],
        [VMEM, anywhere, anywhere, VMEM, VMEM],
        pl.BlockSpec((BQ, HD), lambda i, *s: (i, 0)), jax.ShapeDtypeStruct((seq, HD), BF),
        "two_back", (seq // BQ,), scratch,
    )


def hop(value, pairs):
    heads = lax.axis_size("head")
    table = []
    for source, target in pairs:
        across = int(source // 2 != target // 2)
        table += [(source * heads + h, target * heads + (h ^ across)) for h in range(heads)]
    return lax.ppermute(value, ("group", "head"), table)


def exchange(blocks):
    return lax.all_to_all(blocks, "head", split_axis=0, concat_axis=0, tiled=True)


def shards(queries, keys, values, group_mask, noise_level, token_count, level_gate):
    kv = split_heads(keys[0], values[0])
    query_rows, kv = lax.optimization_barrier((queries[0], kv))
    q = split_heads(query_rows)
    kv = exchange(kv)
    q, kv = lax.optimization_barrier((q, kv))
    q = exchange(q).reshape(-1, HD)
    one = hop(kv, [(0, 1), (1, 2), (2, 3)])
    late, q = lax.optimization_barrier((kv, q))
    far = hop(late, [(0, 2)])
    out = attend(q, kv, one, far, group_mask, noise_level, token_count, level_gate)
    return merge_heads(exchange(out.reshape(kv.shape[0], -1, HD)))[None]


def solution(mesh):
    rows = P("group", "head", None)
    return jax.shard_map(
        shards,
        mesh=mesh,
        in_specs=(rows, rows, rows, P(), P(), P(), P()),
        out_specs=rows,
        check_vma=False,
    )
```

```python
import jax
import jax.numpy as jnp
from jax import lax
from jax.experimental import pallas as pl
from jax.experimental.pallas import tpu as pltpu
from jax.sharding import PartitionSpec as P

HD = 128
NEG = -1e30
SCALE = HD**-0.5 * 1.4426950408889634
LEAST, MOST = 2.0**-80, 2.0**100
BF = jnp.bfloat16
F32 = jnp.float32
VMEM_LIMIT = 40 * 2**20


def params():
    return pltpu.CompilerParams(vmem_limit_bytes=VMEM_LIMIT)


def dot(a, b, ca, cb):
    return lax.dot_general(a, b, (((ca,), (cb,)), ((), ())), preferred_element_type=F32)


def head_block(h):
    return h + (lax.axis_index("group") // 2) * (1 - 2 * (h % 2))


def head_here():
    return head_block(lax.axis_index("head"))


PER = 8
VMEM = pl.BlockSpec(memory_space=pltpu.VMEM)


def split_kernel(*refs):
    rows_refs, out_ref = refs[:-1], refs[-1]
    rows, width = rows_refs[0].shape
    first = pl.program_id(0) * PER
    for h in range(PER):
        for n, ref in enumerate(rows_refs):
            out_ref[first + head_block(h), n * rows : (n + 1) * rows] = ref[:, h * HD : (h + 1) * HD]


def split_heads(*arrays):
    rows, width = arrays[0].shape
    heads = width // HD
    deep = rows * len(arrays)
    return pl.pallas_call(
        split_kernel,
        grid=(heads // PER,),
        in_specs=[pl.BlockSpec((rows, PER * HD), lambda i: (0, i))] * len(arrays),
        out_specs=VMEM,
        out_shape=jax.ShapeDtypeStruct((heads, deep, HD), BF),
        compiler_params=params(),
        name="split_heads",
    )(*arrays)


def merge_kernel(blocks_ref, out_ref):
    first = pl.program_id(0) * PER
    for h in range(PER):
        out_ref[:, h * HD : (h + 1) * HD] = blocks_ref[first + head_block(h)]


def merge_heads(blocks):
    heads, rows, _ = blocks.shape
    return pl.pallas_call(
        merge_kernel,
        grid=(heads // PER,),
        in_specs=[VMEM],
        out_specs=pl.BlockSpec((rows, PER * HD), lambda i: (0, i)),
        out_shape=jax.ShapeDtypeStruct((rows, heads * HD), BF),
        compiler_params=params(),
        name="merge_heads",
    )(blocks)


BQ = 2048
STEP = 4
CHUNK = 8


def key_block(kv_ref, first, blocks):
    return kv_ref[pl.ds(first, blocks), :HD].reshape(blocks * HD, HD)


def value_block(kv_ref, first, blocks):
    return kv_ref[pl.ds(first, blocks), HD:].reshape(blocks * HD, HD)


def unshifted_sums(q, kv_ref, live, first, blocks, masked, l_ref, acc_ref, l_old, acc_old):
    p = jnp.exp2(dot(key_block(kv_ref, first, blocks), q, 1, 1) * SCALE)
    if masked:
        rows = lax.broadcasted_iota(jnp.int32, (blocks * HD, 1), 0) + first * HD
        p = jnp.where(rows < live, p, 0.0)
    l_here = jnp.sum(p, axis=0, keepdims=True)
    acc_here = dot(value_block(kv_ref, first, blocks), p.astype(BF), 0, 0)
    l_ref[...] = l_here if l_old is None else l_old[...] + l_here
    acc_ref[...] = acc_here if acc_old is None else acc_old[...] + acc_here


def shifted_sums(q, kv_ref, live, m_ref, l_ref, acc_ref):
    @pl.loop(0, pl.cdiv(live, HD))
    def _(first):
        s = dot(key_block(kv_ref, first, 1), q, 1, 1) * SCALE
        rows = lax.broadcasted_iota(jnp.int32, (HD, 1), 0) + first * HD
        counted = rows < live
        s = jnp.where(counted, s, NEG)
        old = m_ref[...]
        new = jnp.maximum(old, jnp.max(s, axis=0, keepdims=True))
        p = jnp.where(counted, jnp.exp2(s - new), 0.0)
        shrink = jnp.exp2(old - new)
        m_ref[...] = new
        l_ref[...] = l_ref[...] * shrink + jnp.sum(p, axis=0, keepdims=True)
        acc_ref[...] = acc_ref[...] * shrink + dot(value_block(kv_ref, first, 1), p.astype(BF), 0, 0)


def pair_sums(q, kv_ref, live, old, new):
    m_ref, l_ref, acc_ref = new
    sure = kv_ref.shape[0] // 2
    _, l_old, acc_old = old or (None, None, None)
    unshifted_sums(q, kv_ref, live, 0, sure, False, l_ref, acc_ref, l_old, acc_old)
    whole = (live - sure * HD) // (CHUNK * HD)
    rest = live - (sure + whole * CHUNK) * HD

    @pl.loop(0, whole)
    def _(n):
        first = sure + n * CHUNK
        unshifted_sums(q, kv_ref, live, first, CHUNK, False, l_ref, acc_ref, l_ref, acc_ref)

    @pl.loop(0, pl.cdiv(rest, STEP * HD))
    def _(n):
        first = sure + whole * CHUNK + n * STEP
        unshifted_sums(q, kv_ref, live, first, STEP, True, l_ref, acc_ref, l_ref, acc_ref)

    m_ref[...] = jnp.zeros_like(m_ref) if old is None else old[0][...]
    sums = l_ref[...]
    good = jnp.logical_and(jnp.min(sums) >= LEAST, jnp.max(sums) <= MOST)
    if old is not None:
        good = jnp.logical_and(good, jnp.max(jnp.abs(old[0][...])) == 0.0)

    @pl.when(jnp.logical_not(good))
    def _():
        if old is None:
            m_ref[...] = jnp.full_like(m_ref, NEG)
            l_ref[...] = jnp.zeros_like(l_ref)
            acc_ref[...] = jnp.zeros_like(acc_ref)
        else:
            l_ref[...] = old[1][...]
            acc_ref[...] = old[2][...]
        shifted_sums(q, kv_ref, live, m_ref, l_ref, acc_ref)


DEEP = HD + 8


def parts(ref):
    return ref.at[HD : HD + 1], ref.at[HD + 1 : HD + 2], ref.at[:HD]


def tile(ref, i):
    return ref.at[:, pl.ds(pl.multiple_of(i * BQ, BQ), BQ)]


def query_tile(q_ref, i):
    return q_ref[pl.ds(pl.multiple_of(i * BQ, BQ), BQ), :]


def own_kernel(count_ref, q_ref, kv_ref, new_ref):
    live = count_ref[lax.axis_index("group")]

    @pl.loop(0, q_ref.shape[0] // BQ)
    def _(i):
        pair_sums(query_tile(q_ref, i), kv_ref, live, None, parts(tile(new_ref, i)))


def source_of(mask_ref, offset):
    group = lax.axis_index("group")
    source = jnp.maximum(group - offset, 0)
    return source, jnp.logical_and(group >= offset, mask_ref[group, source, head_here()] == 1)


def one_kernel(count_ref, mask_ref, q_ref, kv_ref, old_ref, new_ref):
    source, active = source_of(mask_ref, 1)

    @pl.loop(0, q_ref.shape[0] // BQ)
    def _(i):
        old, new = tile(old_ref, i), tile(new_ref, i)

        @pl.when(active)
        def _():
            pair_sums(query_tile(q_ref, i), kv_ref, count_ref[source], parts(old), parts(new))

        @pl.when(jnp.logical_not(active))
        def _():
            new[...] = old[...]


def two_kernel(
    count_ref, mask_ref, level_ref, q_ref, near_ref, far_ref, gate_ref, old_ref,
    out_ref, kv_ref, sems, new_ref,
):
    source, active = source_of(mask_ref, 2)
    group = lax.axis_index("group")
    i = pl.program_id(0)
    old = tile(old_ref, i)
    pieces = sems.shape[0]
    deep = kv_ref.shape[0] // pieces

    def copy(ref, n):
        part = pl.ds(n * deep, deep)
        return pltpu.make_async_copy(ref.at[part], kv_ref.at[part], sems.at[n])

    @pl.when(active)
    def _():
        @pl.when(i == 0)
        def _():
            @pl.when(group == 3)
            def _():
                for n in range(pieces):
                    copy(near_ref, n).start()

            @pl.when(group != 3)
            def _():
                for n in range(pieces):
                    copy(far_ref, n).start()

            for n in range(pieces):
                copy(far_ref, n).wait()

        pair_sums(query_tile(q_ref, i), kv_ref, count_ref[source], parts(old), parts(new_ref))

    @pl.when(jnp.logical_not(active))
    def _():
        new_ref[...] = old[...]

    gates = gate_ref[:, pl.ds(pl.multiple_of(head_here() * HD, HD), HD)]
    levels = lax.broadcasted_iota(jnp.int32, gates.shape, 0)
    gate = jnp.sum(jnp.where(levels == level_ref[group], gates, 0.0), axis=0, keepdims=True)
    _, l_ref, acc_ref = parts(new_ref)
    out_ref[...] = ((acc_ref[...] / l_ref[...]).T * gate).astype(BF)


def call(kernel, scalars, operands, in_specs, out_specs, out_shape, name, grid=(1,), scratch=()):
    seq = operands[0].shape[0]
    return pl.pallas_call(
        kernel,
        grid_spec=pltpu.PrefetchScalarGridSpec(
            num_scalar_prefetch=len(scalars),
            grid=grid,
            in_specs=in_specs,
            out_specs=out_specs,
            scratch_shapes=scratch,
        ),
        out_shape=out_shape,
        compiler_params=params(),
        cost_estimate=pl.CostEstimate(
            flops=4 * seq * seq * HD, bytes_accessed=8 * 2**20, transcendentals=seq * seq
        ),
        name=name,
    )(*scalars, *operands)


def attend(q, own, one, far, group_mask, noise_level, token_count, level_gate):
    seq = q.shape[0]
    state = jax.ShapeDtypeStruct((DEEP, seq), F32)
    carried = call(own_kernel, [token_count], [q, own], [VMEM] * 2, VMEM, state, "own_group")
    one, carried = lax.optimization_barrier((one, carried))
    near = hop(one, [(2, 3)])
    carried = call(
        one_kernel, [token_count, group_mask], [q, one, carried], [VMEM] * 3, VMEM, state, "one_back"
    )
    anywhere = pl.BlockSpec(memory_space=pl.ANY)
    scratch = [
        pltpu.VMEM(own.shape, BF),
        pltpu.SemaphoreType.DMA((8,)),
        pltpu.VMEM((DEEP, BQ), F32),
    ]
    return call(
        two_kernel, [token_count, group_mask, noise_level], [q, near, far, level_gate, carried],
        [VMEM, anywhere, anywhere, VMEM, VMEM],
        pl.BlockSpec((BQ, HD), lambda i, *s: (i, 0)), jax.ShapeDtypeStruct((seq, HD), BF),
        "two_back", (seq // BQ,), scratch,
    )


def hop(value, pairs):
    heads = lax.axis_size("head")
    table = []
    for source, target in pairs:
        across = int(source // 2 != target // 2)
        table += [(source * heads + h, target * heads + (h ^ across)) for h in range(heads)]
    return lax.ppermute(value, ("group", "head"), table)


def exchange(blocks):
    return lax.all_to_all(blocks, "head", split_axis=0, concat_axis=0, tiled=True)


def shards(queries, keys, values, group_mask, noise_level, token_count, level_gate):
    kv = split_heads(keys[0], values[0])
    query_rows, kv = lax.optimization_barrier((queries[0], kv))
    q = split_heads(query_rows)
    kv = exchange(kv)
    q, kv = lax.optimization_barrier((q, kv))
    q = exchange(q).reshape(-1, HD)
    one = hop(kv, [(0, 1), (1, 2), (2, 3)])
    late, q = lax.optimization_barrier((kv, q))
    far = hop(late, [(0, 2)])
    out = attend(q, kv, one, far, group_mask, noise_level, token_count, level_gate)
    return merge_heads(exchange(out.reshape(kv.shape[0], -1, HD)))[None]


def solution(mesh):
    rows = P("group", "head", None)
    return jax.shard_map(
        shards,
        mesh=mesh,
        in_specs=(rows, rows, rows, P(), P(), P(), P()),
        out_specs=rows,
        check_vma=False,
    )
```

```python
import jax
import jax.numpy as jnp
from jax import lax
from jax.experimental import pallas as pl
from jax.experimental.pallas import tpu as pltpu
from jax.sharding import PartitionSpec as P

HD = 128
NEG = -1e30
SCALE = HD**-0.5 * 1.4426950408889634
LEAST, MOST = 2.0**-80, 2.0**100
BF = jnp.bfloat16
F32 = jnp.float32
VMEM_LIMIT = 40 * 2**20


def params(limit=VMEM_LIMIT):
    return pltpu.CompilerParams(vmem_limit_bytes=limit)


def dot(a, b, ca, cb):
    return lax.dot_general(a, b, (((ca,), (cb,)), ((), ())), preferred_element_type=F32)


def head_block(h):
    return h + (lax.axis_index("group") // 2) * (1 - 2 * (h % 2))


def head_here():
    return head_block(lax.axis_index("head"))


PER = 8
VMEM = pl.BlockSpec(memory_space=pltpu.VMEM)


PIECE = 16
SPLIT_PER = 4


def split_kernel(*refs):
    rows_refs, (out_ref, held_ref, made_ref, in_sems, out_sems) = refs[:-5], refs[-5:]
    rows = held_ref.shape[1]
    copies = []
    for n, ref in enumerate(rows_refs):
        for p in range(rows // PIECE):
            part = pl.ds(p * PIECE, PIECE)
            copies.append(pltpu.make_async_copy(ref.at[part], held_ref.at[n, part], in_sems.at[n, p]))
    for copy in copies:
        copy.start()
    for copy in copies:
        copy.wait()

    def out_copy(step):
        part = pl.ds(step * SPLIT_PER, SPLIT_PER)
        return pltpu.make_async_copy(made_ref.at[part], out_ref.at[part], out_sems.at[step])

    @pl.loop(0, out_ref.shape[0] // SPLIT_PER)
    def _(step):
        for h in range(SPLIT_PER):
            place = step * SPLIT_PER + h
            columns = pl.ds(pl.multiple_of(place * HD, HD), HD)
            for n in range(len(rows_refs)):
                made_ref[head_block(place), n * rows : (n + 1) * rows] = held_ref[n, :, columns]
        out_copy(step).start()

    @pl.loop(0, out_ref.shape[0] // SPLIT_PER)
    def _(step):
        out_copy(step).wait()


def split_heads(*arrays):
    rows, width = arrays[0].shape
    heads = width // HD
    deep = rows * len(arrays)
    anywhere = pl.BlockSpec(memory_space=pl.ANY)
    return pl.pallas_call(
        split_kernel,
        in_specs=[anywhere] * len(arrays),
        out_specs=anywhere,
        out_shape=jax.ShapeDtypeStruct((heads, deep, HD), BF),
        scratch_shapes=[
            pltpu.VMEM((len(arrays), rows, width), BF),
            pltpu.VMEM((heads, deep, HD), BF),
            pltpu.SemaphoreType.DMA((len(arrays), rows // PIECE)),
            pltpu.SemaphoreType.DMA((heads // SPLIT_PER,)),
        ],
        compiler_params=params(60 * 2**20),
        name="split_heads",
    )(*arrays)


def merge_kernel(blocks_ref, out_ref):
    first = pl.program_id(0) * PER
    for h in range(PER):
        out_ref[:, h * HD : (h + 1) * HD] = blocks_ref[first + head_block(h)]


def merge_heads(blocks):
    heads, rows, _ = blocks.shape
    return pl.pallas_call(
        merge_kernel,
        grid=(heads // PER,),
        in_specs=[VMEM],
        out_specs=pl.BlockSpec((rows, PER * HD), lambda i: (0, i)),
        out_shape=jax.ShapeDtypeStruct((rows, heads * HD), BF),
        compiler_params=params(),
        name="merge_heads",
    )(blocks)


BQ = 2048
STEP = 4
CHUNK = 8


def key_block(kv_ref, first, blocks):
    return kv_ref[pl.ds(first, blocks), :HD].reshape(blocks * HD, HD)


def value_block(kv_ref, first, blocks):
    return kv_ref[pl.ds(first, blocks), HD:].reshape(blocks * HD, HD)


def unshifted_sums(q, kv_ref, live, first, blocks, masked, l_ref, acc_ref, l_old, acc_old):
    p = jnp.exp2(dot(key_block(kv_ref, first, blocks), q, 1, 1) * SCALE)
    if masked:
        rows = lax.broadcasted_iota(jnp.int32, (blocks * HD, 1), 0) + first * HD
        p = jnp.where(rows < live, p, 0.0)
    l_here = jnp.sum(p, axis=0, keepdims=True)
    acc_here = dot(value_block(kv_ref, first, blocks), p.astype(BF), 0, 0)
    l_ref[...] = l_here if l_old is None else l_old[...] + l_here
    acc_ref[...] = acc_here if acc_old is None else acc_old[...] + acc_here


def shifted_sums(q, kv_ref, live, m_ref, l_ref, acc_ref):
    @pl.loop(0, pl.cdiv(live, HD))
    def _(first):
        s = dot(key_block(kv_ref, first, 1), q, 1, 1) * SCALE
        rows = lax.broadcasted_iota(jnp.int32, (HD, 1), 0) + first * HD
        counted = rows < live
        s = jnp.where(counted, s, NEG)
        old = m_ref[...]
        new = jnp.maximum(old, jnp.max(s, axis=0, keepdims=True))
        p = jnp.where(counted, jnp.exp2(s - new), 0.0)
        shrink = jnp.exp2(old - new)
        m_ref[...] = new
        l_ref[...] = l_ref[...] * shrink + jnp.sum(p, axis=0, keepdims=True)
        acc_ref[...] = acc_ref[...] * shrink + dot(value_block(kv_ref, first, 1), p.astype(BF), 0, 0)


def pair_sums(q, kv_ref, live, old, new):
    m_ref, l_ref, acc_ref = new
    sure = kv_ref.shape[0] // 2
    _, l_old, acc_old = old or (None, None, None)
    unshifted_sums(q, kv_ref, live, 0, sure, False, l_ref, acc_ref, l_old, acc_old)
    whole = (live - sure * HD) // (CHUNK * HD)
    rest = live - (sure + whole * CHUNK) * HD

    for count in range(1, sure // CHUNK + 1):

        @pl.when(whole == count)
        def _():
            blocks = count * CHUNK
            unshifted_sums(q, kv_ref, live, sure, blocks, False, l_ref, acc_ref, l_ref, acc_ref)

    @pl.loop(0, pl.cdiv(rest, STEP * HD))
    def _(n):
        first = sure + whole * CHUNK + n * STEP
        unshifted_sums(q, kv_ref, live, first, STEP, True, l_ref, acc_ref, l_ref, acc_ref)

    m_ref[...] = jnp.zeros_like(m_ref) if old is None else old[0][...]
    sums = l_ref[...]
    good = jnp.logical_and(jnp.min(sums) >= LEAST, jnp.max(sums) <= MOST)
    if old is not None:
        good = jnp.logical_and(good, jnp.max(jnp.abs(old[0][...])) == 0.0)

    @pl.when(jnp.logical_not(good))
    def _():
        if old is None:
            m_ref[...] = jnp.full_like(m_ref, NEG)
            l_ref[...] = jnp.zeros_like(l_ref)
            acc_ref[...] = jnp.zeros_like(acc_ref)
        else:
            l_ref[...] = old[1][...]
            acc_ref[...] = old[2][...]
        shifted_sums(q, kv_ref, live, m_ref, l_ref, acc_ref)


DEEP = HD + 8


def parts(ref):
    return ref.at[HD : HD + 1], ref.at[HD + 1 : HD + 2], ref.at[:HD]


def tile(ref, i):
    return ref.at[:, pl.ds(pl.multiple_of(i * BQ, BQ), BQ)]


def query_tile(q_ref, i):
    return q_ref[pl.ds(pl.multiple_of(i * BQ, BQ), BQ), :]


def own_kernel(count_ref, q_ref, kv_ref, new_ref):
    live = count_ref[lax.axis_index("group")]

    @pl.loop(0, q_ref.shape[0] // BQ)
    def _(i):
        pair_sums(query_tile(q_ref, i), kv_ref, live, None, parts(tile(new_ref, i)))


def source_of(mask_ref, offset):
    group = lax.axis_index("group")
    source = jnp.maximum(group - offset, 0)
    return source, jnp.logical_and(group >= offset, mask_ref[group, source, head_here()] == 1)


def one_kernel(count_ref, mask_ref, q_ref, kv_ref, old_ref, new_ref):
    source, active = source_of(mask_ref, 1)

    @pl.loop(0, q_ref.shape[0] // BQ)
    def _(i):
        old, new = tile(old_ref, i), tile(new_ref, i)

        @pl.when(active)
        def _():
            pair_sums(query_tile(q_ref, i), kv_ref, count_ref[source], parts(old), parts(new))

        @pl.when(jnp.logical_not(active))
        def _():
            new[...] = old[...]


def two_kernel(
    count_ref, mask_ref, level_ref, q_ref, near_ref, far_ref, gate_ref, old_ref,
    out_ref, kv_ref, sems, new_ref,
):
    source, active = source_of(mask_ref, 2)
    group = lax.axis_index("group")
    i = pl.program_id(0)
    old = tile(old_ref, i)
    pieces = sems.shape[0]
    deep = kv_ref.shape[0] // pieces

    def copy(ref, n):
        part = pl.ds(n * deep, deep)
        return pltpu.make_async_copy(ref.at[part], kv_ref.at[part], sems.at[n])

    @pl.when(active)
    def _():
        @pl.when(i == 0)
        def _():
            @pl.when(group == 3)
            def _():
                for n in range(pieces):
                    copy(near_ref, n).start()

            @pl.when(group != 3)
            def _():
                for n in range(pieces):
                    copy(far_ref, n).start()

            for n in range(pieces):
                copy(far_ref, n).wait()

        pair_sums(query_tile(q_ref, i), kv_ref, count_ref[source], parts(old), parts(new_ref))

    @pl.when(jnp.logical_not(active))
    def _():
        new_ref[...] = old[...]

    gates = gate_ref[:, pl.ds(pl.multiple_of(head_here() * HD, HD), HD)]
    levels = lax.broadcasted_iota(jnp.int32, gates.shape, 0)
    gate = jnp.sum(jnp.where(levels == level_ref[group], gates, 0.0), axis=0, keepdims=True)
    _, l_ref, acc_ref = parts(new_ref)
    out_ref[...] = ((acc_ref[...] / l_ref[...]).T * gate).astype(BF)


def call(kernel, scalars, operands, in_specs, out_specs, out_shape, name, grid=(1,), scratch=()):
    seq = operands[0].shape[0]
    return pl.pallas_call(
        kernel,
        grid_spec=pltpu.PrefetchScalarGridSpec(
            num_scalar_prefetch=len(scalars),
            grid=grid,
            in_specs=in_specs,
            out_specs=out_specs,
            scratch_shapes=scratch,
        ),
        out_shape=out_shape,
        compiler_params=params(),
        cost_estimate=pl.CostEstimate(
            flops=4 * seq * seq * HD, bytes_accessed=8 * 2**20, transcendentals=seq * seq
        ),
        name=name,
    )(*scalars, *operands)


def attend(q, own, one, far, group_mask, noise_level, token_count, level_gate):
    seq = q.shape[0]
    state = jax.ShapeDtypeStruct((DEEP, seq), F32)
    carried = call(own_kernel, [token_count], [q, own], [VMEM] * 2, VMEM, state, "own_group")
    one, carried = lax.optimization_barrier((one, carried))
    near = hop(one, [(2, 3)])
    carried = call(
        one_kernel, [token_count, group_mask], [q, one, carried], [VMEM] * 3, VMEM, state, "one_back"
    )
    anywhere = pl.BlockSpec(memory_space=pl.ANY)
    scratch = [
        pltpu.VMEM(own.shape, BF),
        pltpu.SemaphoreType.DMA((8,)),
        pltpu.VMEM((DEEP, BQ), F32),
    ]
    return call(
        two_kernel, [token_count, group_mask, noise_level], [q, near, far, level_gate, carried],
        [VMEM, anywhere, anywhere, VMEM, VMEM],
        pl.BlockSpec((BQ, HD), lambda i, *s: (i, 0)), jax.ShapeDtypeStruct((seq, HD), BF),
        "two_back", (seq // BQ,), scratch,
    )


def hop(value, pairs):
    heads = lax.axis_size("head")
    table = []
    for source, target in pairs:
        across = int(source // 2 != target // 2)
        table += [(source * heads + h, target * heads + (h ^ across)) for h in range(heads)]
    return lax.ppermute(value, ("group", "head"), table)


def exchange(blocks):
    return lax.all_to_all(blocks, "head", split_axis=0, concat_axis=0, tiled=True)


def shards(queries, keys, values, group_mask, noise_level, token_count, level_gate):
    kv = split_heads(keys[0], values[0])
    query_rows, kv = lax.optimization_barrier((queries[0], kv))
    q = split_heads(query_rows)
    kv = exchange(kv)
    q, kv = lax.optimization_barrier((q, kv))
    q = exchange(q).reshape(-1, HD)
    one = hop(kv, [(0, 1), (1, 2), (2, 3)])
    late, q = lax.optimization_barrier((kv, q))
    far = hop(late, [(0, 2)])
    out = attend(q, kv, one, far, group_mask, noise_level, token_count, level_gate)
    return merge_heads(exchange(out.reshape(kv.shape[0], -1, HD)))[None]


def solution(mesh):
    rows = P("group", "head", None)
    return jax.shard_map(
        shards,
        mesh=mesh,
        in_specs=(rows, rows, rows, P(), P(), P(), P()),
        out_specs=rows,
        check_vma=False,
    )
```

```python
import jax
import jax.numpy as jnp
from jax import lax
from jax.experimental import pallas as pl
from jax.experimental.pallas import tpu as pltpu
from jax.sharding import PartitionSpec as P

HD = 128
NEG = -1e30
SCALE = HD**-0.5 * 1.4426950408889634
LEAST, MOST = 2.0**-80, 2.0**100
BF = jnp.bfloat16
F32 = jnp.float32
VMEM_LIMIT = 40 * 2**20


def params(limit=VMEM_LIMIT):
    return pltpu.CompilerParams(vmem_limit_bytes=limit)


def dot(a, b, ca, cb):
    return lax.dot_general(a, b, (((ca,), (cb,)), ((), ())), preferred_element_type=F32)


def head_block(h):
    return h + (lax.axis_index("group") // 2) * (1 - 2 * (h % 2))


def head_here():
    return head_block(lax.axis_index("head"))


PER = 8
VMEM = pl.BlockSpec(memory_space=pltpu.VMEM)


PIECE = 16
SPLIT_PER = 4


def split_kernel(*refs):
    rows_refs, (out_ref, held_ref, made_ref, in_sems, out_sems) = refs[:-5], refs[-5:]
    rows = held_ref.shape[1]
    copies = []
    for n, ref in enumerate(rows_refs):
        for p in range(rows // PIECE):
            part = pl.ds(p * PIECE, PIECE)
            copies.append(pltpu.make_async_copy(ref.at[part], held_ref.at[n, part], in_sems.at[n, p]))
    for copy in copies:
        copy.start()
    for copy in copies:
        copy.wait()

    def out_copy(step):
        part = pl.ds(step * SPLIT_PER, SPLIT_PER)
        return pltpu.make_async_copy(made_ref.at[part], out_ref.at[part], out_sems.at[step])

    @pl.loop(0, out_ref.shape[0] // SPLIT_PER)
    def _(step):
        for h in range(SPLIT_PER):
            place = step * SPLIT_PER + h
            columns = pl.ds(pl.multiple_of(place * HD, HD), HD)
            for n in range(len(rows_refs)):
                made_ref[head_block(place), n * rows : (n + 1) * rows] = held_ref[n, :, columns]
        out_copy(step).start()

    @pl.loop(0, out_ref.shape[0] // SPLIT_PER)
    def _(step):
        out_copy(step).wait()


def split_heads(*arrays):
    rows, width = arrays[0].shape
    heads = width // HD
    deep = rows * len(arrays)
    anywhere = pl.BlockSpec(memory_space=pl.ANY)
    return pl.pallas_call(
        split_kernel,
        in_specs=[anywhere] * len(arrays),
        out_specs=anywhere,
        out_shape=jax.ShapeDtypeStruct((heads, deep, HD), BF),
        scratch_shapes=[
            pltpu.VMEM((len(arrays), rows, width), BF),
            pltpu.VMEM((heads, deep, HD), BF),
            pltpu.SemaphoreType.DMA((len(arrays), rows // PIECE)),
            pltpu.SemaphoreType.DMA((heads // SPLIT_PER,)),
        ],
        compiler_params=params(60 * 2**20),
        name="split_heads",
    )(*arrays)


def merge_kernel(blocks_ref, out_ref):
    first = pl.program_id(0) * PER
    for h in range(PER):
        out_ref[:, h * HD : (h + 1) * HD] = blocks_ref[first + head_block(h)]


def merge_heads(blocks):
    heads, rows, _ = blocks.shape
    return pl.pallas_call(
        merge_kernel,
        grid=(heads // PER,),
        in_specs=[VMEM],
        out_specs=pl.BlockSpec((rows, PER * HD), lambda i: (0, i)),
        out_shape=jax.ShapeDtypeStruct((rows, heads * HD), BF),
        compiler_params=params(),
        name="merge_heads",
    )(blocks)


BQ = 2048
STEP = 4
CHUNK = 8


def key_block(kv_ref, first, blocks):
    return kv_ref[pl.ds(first, blocks), :HD].reshape(blocks * HD, HD)


def value_block(kv_ref, first, blocks):
    return kv_ref[pl.ds(first, blocks), HD:].reshape(blocks * HD, HD)


def unshifted_sums(q, kv_ref, live, first, blocks, masked, l_ref, acc_ref, l_old, acc_old):
    p = jnp.exp2(dot(key_block(kv_ref, first, blocks), q, 1, 1) * SCALE)
    if masked:
        rows = lax.broadcasted_iota(jnp.int32, (blocks * HD, 1), 0) + first * HD
        p = jnp.where(rows < live, p, 0.0)
    l_here = jnp.sum(p, axis=0, keepdims=True)
    acc_here = dot(value_block(kv_ref, first, blocks), p.astype(BF), 0, 0)
    l_ref[...] = l_here if l_old is None else l_old[...] + l_here
    acc_ref[...] = acc_here if acc_old is None else acc_old[...] + acc_here


def shifted_sums(q, kv_ref, live, m_ref, l_ref, acc_ref):
    @pl.loop(0, pl.cdiv(live, HD))
    def _(first):
        s = dot(key_block(kv_ref, first, 1), q, 1, 1) * SCALE
        rows = lax.broadcasted_iota(jnp.int32, (HD, 1), 0) + first * HD
        counted = rows < live
        s = jnp.where(counted, s, NEG)
        old = m_ref[...]
        new = jnp.maximum(old, jnp.max(s, axis=0, keepdims=True))
        p = jnp.where(counted, jnp.exp2(s - new), 0.0)
        shrink = jnp.exp2(old - new)
        m_ref[...] = new
        l_ref[...] = l_ref[...] * shrink + jnp.sum(p, axis=0, keepdims=True)
        acc_ref[...] = acc_ref[...] * shrink + dot(value_block(kv_ref, first, 1), p.astype(BF), 0, 0)


def pair_sums(q, kv_ref, live, old, new):
    m_ref, l_ref, acc_ref = new
    sure = kv_ref.shape[0] // 2
    _, l_old, acc_old = old or (None, None, None)
    unshifted_sums(q, kv_ref, live, 0, sure, False, l_ref, acc_ref, l_old, acc_old)
    whole = (live - sure * HD) // (CHUNK * HD)
    rest = live - (sure + whole * CHUNK) * HD

    for count in range(1, sure // CHUNK + 1):

        @pl.when(whole == count)
        def _():
            blocks = count * CHUNK
            unshifted_sums(q, kv_ref, live, sure, blocks, False, l_ref, acc_ref, l_ref, acc_ref)

    for count in range(1, CHUNK // STEP + 1):

        @pl.when(pl.cdiv(rest, STEP * HD) == count)
        def _():
            first = sure + whole * CHUNK
            blocks = count * STEP
            unshifted_sums(q, kv_ref, live, first, blocks, True, l_ref, acc_ref, l_ref, acc_ref)

    m_ref[...] = jnp.zeros_like(m_ref) if old is None else old[0][...]
    sums = l_ref[...]
    good = jnp.logical_and(jnp.min(sums) >= LEAST, jnp.max(sums) <= MOST)
    if old is not None:
        good = jnp.logical_and(good, jnp.max(jnp.abs(old[0][...])) == 0.0)

    @pl.when(jnp.logical_not(good))
    def _():
        if old is None:
            m_ref[...] = jnp.full_like(m_ref, NEG)
            l_ref[...] = jnp.zeros_like(l_ref)
            acc_ref[...] = jnp.zeros_like(acc_ref)
        else:
            l_ref[...] = old[1][...]
            acc_ref[...] = old[2][...]
        shifted_sums(q, kv_ref, live, m_ref, l_ref, acc_ref)


DEEP = HD + 8


def parts(ref):
    return ref.at[HD : HD + 1], ref.at[HD + 1 : HD + 2], ref.at[:HD]


def tile(ref, i):
    return ref.at[:, pl.ds(pl.multiple_of(i * BQ, BQ), BQ)]


def query_tile(q_ref, i):
    return q_ref[pl.ds(pl.multiple_of(i * BQ, BQ), BQ), :]


def own_kernel(count_ref, q_ref, kv_ref, new_ref):
    live = count_ref[lax.axis_index("group")]

    @pl.loop(0, q_ref.shape[0] // BQ)
    def _(i):
        pair_sums(query_tile(q_ref, i), kv_ref, live, None, parts(tile(new_ref, i)))


def source_of(mask_ref, offset):
    group = lax.axis_index("group")
    source = jnp.maximum(group - offset, 0)
    return source, jnp.logical_and(group >= offset, mask_ref[group, source, head_here()] == 1)


def one_kernel(count_ref, mask_ref, q_ref, kv_ref, old_ref, new_ref):
    source, active = source_of(mask_ref, 1)

    @pl.loop(0, q_ref.shape[0] // BQ)
    def _(i):
        old, new = tile(old_ref, i), tile(new_ref, i)

        @pl.when(active)
        def _():
            pair_sums(query_tile(q_ref, i), kv_ref, count_ref[source], parts(old), parts(new))

        @pl.when(jnp.logical_not(active))
        def _():
            new[...] = old[...]


def two_kernel(
    count_ref, mask_ref, level_ref, q_ref, near_ref, far_ref, gate_ref, old_ref,
    out_ref, kv_ref, sems, new_ref,
):
    source, active = source_of(mask_ref, 2)
    group = lax.axis_index("group")
    i = pl.program_id(0)
    old = tile(old_ref, i)
    pieces = sems.shape[0]
    deep = kv_ref.shape[0] // pieces

    def copy(ref, n):
        part = pl.ds(n * deep, deep)
        return pltpu.make_async_copy(ref.at[part], kv_ref.at[part], sems.at[n])

    @pl.when(active)
    def _():
        @pl.when(i == 0)
        def _():
            @pl.when(group == 3)
            def _():
                for n in range(pieces):
                    copy(near_ref, n).start()

            @pl.when(group != 3)
            def _():
                for n in range(pieces):
                    copy(far_ref, n).start()

            for n in range(pieces):
                copy(far_ref, n).wait()

        pair_sums(query_tile(q_ref, i), kv_ref, count_ref[source], parts(old), parts(new_ref))

    @pl.when(jnp.logical_not(active))
    def _():
        new_ref[...] = old[...]

    gates = gate_ref[:, pl.ds(pl.multiple_of(head_here() * HD, HD), HD)]
    levels = lax.broadcasted_iota(jnp.int32, gates.shape, 0)
    gate = jnp.sum(jnp.where(levels == level_ref[group], gates, 0.0), axis=0, keepdims=True)
    _, l_ref, acc_ref = parts(new_ref)
    out_ref[...] = ((acc_ref[...] / l_ref[...]).T * gate).astype(BF)


def call(kernel, scalars, operands, in_specs, out_specs, out_shape, name, grid=(1,), scratch=()):
    seq = operands[0].shape[0]
    return pl.pallas_call(
        kernel,
        grid_spec=pltpu.PrefetchScalarGridSpec(
            num_scalar_prefetch=len(scalars),
            grid=grid,
            in_specs=in_specs,
            out_specs=out_specs,
            scratch_shapes=scratch,
        ),
        out_shape=out_shape,
        compiler_params=params(),
        cost_estimate=pl.CostEstimate(
            flops=4 * seq * seq * HD, bytes_accessed=8 * 2**20, transcendentals=seq * seq
        ),
        name=name,
    )(*scalars, *operands)


def attend(q, own, one, far, group_mask, noise_level, token_count, level_gate):
    seq = q.shape[0]
    state = jax.ShapeDtypeStruct((DEEP, seq), F32)
    carried = call(own_kernel, [token_count], [q, own], [VMEM] * 2, VMEM, state, "own_group")
    one, carried = lax.optimization_barrier((one, carried))
    near = hop(one, [(2, 3)])
    carried = call(
        one_kernel, [token_count, group_mask], [q, one, carried], [VMEM] * 3, VMEM, state, "one_back"
    )
    anywhere = pl.BlockSpec(memory_space=pl.ANY)
    scratch = [
        pltpu.VMEM(own.shape, BF),
        pltpu.SemaphoreType.DMA((8,)),
        pltpu.VMEM((DEEP, BQ), F32),
    ]
    return call(
        two_kernel, [token_count, group_mask, noise_level], [q, near, far, level_gate, carried],
        [VMEM, anywhere, anywhere, VMEM, VMEM],
        pl.BlockSpec((BQ, HD), lambda i, *s: (i, 0)), jax.ShapeDtypeStruct((seq, HD), BF),
        "two_back", (seq // BQ,), scratch,
    )


def hop(value, pairs):
    heads = lax.axis_size("head")
    table = []
    for source, target in pairs:
        across = int(source // 2 != target // 2)
        table += [(source * heads + h, target * heads + (h ^ across)) for h in range(heads)]
    return lax.ppermute(value, ("group", "head"), table)


def exchange(blocks):
    return lax.all_to_all(blocks, "head", split_axis=0, concat_axis=0, tiled=True)


def shards(queries, keys, values, group_mask, noise_level, token_count, level_gate):
    kv = split_heads(keys[0], values[0])
    query_rows, kv = lax.optimization_barrier((queries[0], kv))
    q = split_heads(query_rows)
    kv = exchange(kv)
    q, kv = lax.optimization_barrier((q, kv))
    q = exchange(q).reshape(-1, HD)
    one = hop(kv, [(0, 1), (1, 2), (2, 3)])
    late, q = lax.optimization_barrier((kv, q))
    far = hop(late, [(0, 2)])
    out = attend(q, kv, one, far, group_mask, noise_level, token_count, level_gate)
    return merge_heads(exchange(out.reshape(kv.shape[0], -1, HD)))[None]


def solution(mesh):
    rows = P("group", "head", None)
    return jax.shard_map(
        shards,
        mesh=mesh,
        in_specs=(rows, rows, rows, P(), P(), P(), P()),
        out_specs=rows,
        check_vma=False,
    )
```
